128 devices in a mesh: dp: 16 (over z, y_hi, core), layer: 8 (over x, y_lo).
Axes of the slice: x: 4, y: 4 (y_hi: 2, y_lo: 2; y = y_hi * 2 + y_lo), z: 4, core: 2. Of those that a mesh axis runs over, the one named last changes fastest.
Arguments:
- grads_proj: bfloat16 [8, 4096, 64, 256], P('layer', 'dp'), may hold values from -6 to 6
- inputs_proj: bfloat16 [8, 4096, 64, 256], P('layer', 'dp'), may hold values from -6 to 6
Outputs:
- gram: float32 [4096, 4096], P('dp', 'layer')
The draws below stay inside these ranges and needn't reach their ends.
All inputs are finite; a program needn't handle non-finite values.
Results may differ from the reference program's by a relative error of at most 0.002.
Values may be sent and summed in bfloat16 or wider, within the bound.
No kernel may reach another device: no remote copies, remote signals or barrier semaphores. Data moves between devices by JAX's collectives and lax.ppermute only.
A program may use at most 128 MiB of HBM per device.

```python
import jax
import jax.numpy as jnp
from jax import lax

RANK = 64
FEAT = 4096
LAYERS = 8
EXAMPLES = 4096
TOK = 256


def block_levels(rng, extent, cuts, smallest, high):
    level, own = 1.0, jax.random.fold_in(rng, 6)
    for axis_at, parts in cuts:
        steps = jnp.exp(jax.random.uniform(jax.random.fold_in(own, axis_at), (parts,), jnp.float32, smallest / len(cuts), high / len(cuts)))
        level = level * jnp.repeat(steps, extent[axis_at] // parts).reshape([-1 if axis == axis_at else 1 for axis in range(len(extent))])
    return level


def scatter_about(own_key, shape, scale, most, cuts=(), dtype=jnp.bfloat16):
    loudness = block_levels(own_key, shape, cuts, -0.22, 0.18) if cuts else 1.0
    result = jax.random.normal(own_key, shape, jnp.float32) * scale * loudness
    return jnp.minimum(jnp.maximum(result, -most), most).astype(dtype)


def setup_inputs(seed: int = 0) -> dict:
    keys = jax.random.split(jax.random.key(seed), 3)
    grads_proj = scatter_about(keys[0], (LAYERS, EXAMPLES, RANK, TOK), 1.0, 6.0, ((0, 8), (1, 16)))
    inputs_proj = scatter_about(keys[1], (LAYERS, EXAMPLES, RANK, TOK), 1.0, 6.0, ((0, 8), (1, 16)))
    return {"grads_proj": grads_proj, "inputs_proj": inputs_proj}


def reference(grads_proj, inputs_proj):

    def layer_features(pair):
        outs, ins = pair
        prod = jnp.einsum('eot,eit->eoi', outs.astype(jnp.float32), inputs_proj_cast(ins))
        prod = prod * (1.0 / jnp.sqrt(jnp.float32(TOK)))
        return prod.astype(jnp.bfloat16).reshape(EXAMPLES, FEAT)
    stacked = lax.map(layer_features, (grads_proj, inputs_proj))
    features = jnp.transpose(stacked, (1, 0, 2)).reshape(EXAMPLES, LAYERS * FEAT)
    wide = features.astype(jnp.float32)
    product = jnp.dot(wide, wide.T, precision=lax.Precision.HIGHEST)
    return product * (1.0 / jnp.sqrt(jnp.float32(LAYERS * FEAT)))

def inputs_proj_cast(ins):
    return ins.astype(jnp.float32)
```

```python
import functools
import jax
import jax.numpy as jnp
from jax import lax
from jax.experimental import pallas as pl
from jax.experimental.pallas import tpu as pltpu
from jax.sharding import PartitionSpec as P

NT = (((1,), (1,)), ((), ()))

def feat_kernel(core_ref, g_ref, i_ref, fc_ref, fo_ref, prod, *, group, mode):
    n = g_ref.shape[1]
    c = core_ref[0]
    scale = 1.0 / 16.0
    if mode == "dup":
        for e in range(n):
            right = jnp.concatenate([i_ref[0, e], i_ref[0, e]], axis=0)
            prod[pl.ds(e * 64, 64), :] = lax.dot_general(g_ref[0, e], right, NT, preferred_element_type=jnp.float32)
    elif mode == "pair":
        for e in range(0, n, 2):
            right = jnp.concatenate([i_ref[0, e], i_ref[0, e], i_ref[0, e + 1], i_ref[0, e + 1]], axis=0)
            left = jnp.concatenate([g_ref[0, e], g_ref[0, e + 1]], axis=0)
            r = lax.dot_general(left, right, NT, preferred_element_type=jnp.float32)
            prod[pl.ds(e * 64, 64), :] = r[:64, :128]
            prod[pl.ds(e * 64 + 64, 64), :] = r[64:, 128:]
    lane = lax.broadcasted_iota(jnp.int32, (n, 128), 1) < 64
    for half, out in ((c, fc_ref), (1 - c, fo_ref)):
        for t in range(16):
            lo = prod[pl.ds(half * 32 + 2 * t, n, stride=64), :]
            hi = prod[pl.ds(half * 32 + 2 * t + 1, n, stride=64), :]
            out[t] = (jnp.where(lane, lo, hi) * scale).astype(jnp.bfloat16)

def features(core, g, i, n=32, mode="dup"):
    ex = g.shape[1]
    return pl.pallas_call(
        functools.partial(feat_kernel, group=1, mode=mode),
        grid_spec=pltpu.PrefetchScalarGridSpec(
            num_scalar_prefetch=1, grid=(ex // n,),
            in_specs=[pl.BlockSpec((1, n, 64, 256), lambda s, c: (0, s, 0, 0))] * 2,
            out_specs=[pl.BlockSpec((16, n, 128), lambda s, c: (0, s, 0))] * 2,
            scratch_shapes=[pltpu.VMEM((n * 64, 128), jnp.float32)]),
        out_shape=[jax.ShapeDtypeStruct((16, ex, 128), jnp.bfloat16)] * 2,
        compiler_params=pltpu.CompilerParams(vmem_limit_bytes=48 << 20),
        cost_estimate=pl.CostEstimate(flops=2 * ex * 64 * 64 * 256, bytes_accessed=18 << 20, transcendentals=0),
        name="features",
    )(core, g, i)

def cat(ref, lo, n):
    return jnp.concatenate([ref[lo + t] for t in range(n)], axis=1)

def gram_kernel(s_ref, ac, ao, fc, fo, gc, go, xsa, xsb, xoa, xob, x2s, x2o, p0, p1, p2, p3):
    f32 = jnp.float32
    dot = lambda a, b: lax.dot_general(a, b, NT, preferred_element_type=f32)
    outs = (p0, p1, p2, p3)
    def put(which, col, val):
        for d in range(4):
            @pl.when(s_ref[which] == d)
            def _():
                outs[d][:, col * 256:(col + 1) * 256] = val.astype(outs[d].dtype)
    a, b = cat(ac, 0, 16), cat(ao, 0, 16)
    put(0, 0, dot(a, cat(fc, 0, 16)) + dot(b, cat(fo, 0, 16)))
    put(0, 1, dot(a, cat(gc, 0, 16)) + dot(b, cat(go, 0, 16)))
    put(1, 0, dot(a, cat(xsa, 0, 16)))
    put(1, 1, dot(a, cat(xsb, 0, 16)))
    put(2, 0, dot(b, cat(xob, 0, 16)))
    put(2, 1, dot(b, cat(xoa, 0, 16)))
    h = s_ref[4] * 8
    a, b = cat(ac, h, 8), cat(ao, h, 8)
    put(3, 0, dot(a, cat(x2s.at[0], 0, 8)) + dot(b, cat(x2o.at[1], 0, 8)))
    put(3, 1, dot(a, cat(x2s.at[1], 0, 8)) + dot(b, cat(x2o.at[0], 0, 8)))

def gram(slots, *ops):
    rows = ops[0].shape[1]
    v = pl.BlockSpec(memory_space=pltpu.VMEM)
    return pl.pallas_call(
        gram_kernel,
        in_specs=[pl.BlockSpec(memory_space=pltpu.SMEM)] + [v] * len(ops),
        out_specs=[v] * 4,
        out_shape=[jax.ShapeDtypeStruct((rows, 512), jnp.float32)] + [jax.ShapeDtypeStruct((rows, 512), jnp.bfloat16)] * 3,
        compiler_params=pltpu.CompilerParams(vmem_limit_bytes=48 << 20),
        cost_estimate=pl.CostEstimate(flops=2 * rows * 512 * 10240, bytes_accessed=12 << 20, transcendentals=0),
        name="gram",
    )(slots, *ops)


AXES = ("dp", "layer")


def device(x, y, z, c):
    x, y, z = x % 4, y % 4, z % 4
    return ((z * 2 + y // 2) * 2 + c) * 8 + x * 2 + y % 2


def shift(array, move):
    pairs = []
    for x in range(4):
        for y in range(4):
            for z in range(4):
                for c in range(2):
                    place = move(x, y, z, c)
                    if place is not None:
                        pairs.append((device(x, y, z, c), device(*place)))
    return lax.ppermute(array, AXES, pairs)


def other_core(x, y, z, c):
    return x, y, z, 1 - c


def other_half(x, y, z, c):
    return x, y + 2, z, c


def along_z(x, y, z, c):
    return x, y, z - 1 + 2 * c, c


def body(grads_proj, inputs_proj):
    dp = lax.axis_index("dp").astype(jnp.int32)
    layer = lax.axis_index("layer").astype(jnp.int32)
    core = dp % 2
    z = dp // 4
    y = (dp // 2) % 2 * 2 + layer % 2
    x = layer // 2

    own_c, own_o = features(core.reshape(1), grads_proj, inputs_proj)
    far_c, far_o = shift(own_c, other_half), shift(own_o, other_half)
    mate_c = shift(own_o, other_core)
    side_a = shift(own_c, along_z)
    side_b = shift(mate_c, along_z)
    mate_o = shift(own_c, other_core)
    to_z = (z - 1 + 2 * core) % 4
    start = to_z // 2 * 8
    part = jnp.stack([lax.dynamic_slice_in_dim(side_a, start, 8, 0), lax.dynamic_slice_in_dim(side_b, start, 8, 0)])
    two = shift(part, along_z)
    back_a, back_b = shift(side_a, other_core), shift(side_b, other_core)
    two_back = shift(two, other_core)

    near = jnp.where(core == 0, 1, 3)
    slots = jnp.stack([z - x, z + near - x, z + 4 - near - x, z + 2 - x]) % 4
    slots = jnp.concatenate([slots, (z // 2).reshape(1)]).astype(jnp.int32)
    columns = (own_c, own_o, mate_c, mate_o, side_a, side_b, back_a, back_b, two, two_back)

    def over_x(rows_c, rows_o):
        keep, up, two_up, down = gram(slots, rows_c, rows_o, *columns)
        up = shift(up, lambda x, y, z, c: (x + 1, y, z, c))
        down = shift(down, lambda x, y, z, c: (x - 1, y, z, c))
        two_up = shift(two_up, lambda x, y, z, c: (x + 2, y, z, c))
        f32 = jnp.float32
        return (keep + up.astype(f32)) + (down.astype(f32) + two_up.astype(f32))

    near_sum = over_x(own_c, own_o)
    far_sum = over_x(far_c, far_o)
    edge = (y == 0) | (y == 3)
    give = jnp.where(edge, far_sum, near_sum).astype(jnp.bfloat16)
    keep = jnp.where(edge, near_sum, far_sum)
    total = keep + shift(give, lambda x, y, z, c: (x, y ^ 1, z, c)).astype(jnp.float32)
    sent = total.astype(jnp.bfloat16)
    direct = shift(sent, lambda x, y, z, c: (x, 3 - y, z, c) if y in (1, 2) else None).astype(jnp.float32)
    direct = jnp.where(edge, total, direct)
    turn_a = shift(sent[:, :256], lambda x, y, z, c: (z, y, x, c) if x != z else None)
    turn_b = shift(sent[:, 256:], lambda x, y, z, c: (z, y, x, 1 - c) if x != z else None)
    turned = jnp.concatenate([turn_a.T, turn_b.T], axis=1).astype(jnp.float32)
    out = direct + turned
    out = jnp.where(core == 0, out, jnp.concatenate([out[:, 256:], out[:, :256]], axis=1))
    return out * (1.0 / jnp.sqrt(jnp.float32(8 * 4096)))


def solution(mesh):
    return jax.shard_map(
        body,
        mesh=mesh,
        in_specs=(P("layer", "dp", None, None), P("layer", "dp", None, None)),
        out_specs=P("dp", "layer"),
        check_vma=False,
    )
```

```python
import functools
import jax
import jax.numpy as jnp
from jax import lax
from jax.experimental import pallas as pl
from jax.experimental.pallas import tpu as pltpu
from jax.sharding import PartitionSpec as P

NT = (((1,), (1,)), ((), ()))
AXES = ("dp", "layer")
HALF = 16
PITCH = 68


def feature_kernel(core_ref, g_ref, i_ref, out_ref, prod):
    n = g_ref.shape[1]
    core = core_ref[0]
    for e in range(0, n, 4):
        four = lax.dot_general(
            g_ref[0, e : e + 4].reshape(256, 256),
            i_ref[0, e : e + 4].reshape(256, 256),
            NT,
            preferred_element_type=jnp.float32,
        )
        for k in range(4):
            prod[pl.ds((e + k) * PITCH, 64), :] = four[64 * k : 64 * k + 64, 128 * (k // 2) : 128 * (k // 2) + 128]
    even = lax.broadcasted_iota(jnp.int32, (n, 128), 0) % 2 == 0
    left = lax.broadcasted_iota(jnp.int32, (n, 128), 1) < 64
    in_place = even == left
    for part, half in ((0, core), (1, 1 - core)):
        for t in range(HALF):
            first = prod[pl.ds(half * 32 + 2 * t, n, stride=PITCH), :]
            second = prod[pl.ds(half * 32 + 2 * t + 1, n, stride=PITCH), :]
            moved = pltpu.roll(jnp.where(even, second, first), 64, 1)
            out_ref[part * HALF + t] = jnp.where(in_place, jnp.where(even, first, second), moved).astype(jnp.bfloat16)


def features(core, g, i, start, count, n=64):
    skip = start // n
    return pl.pallas_call(
        feature_kernel,
        grid_spec=pltpu.PrefetchScalarGridSpec(
            num_scalar_prefetch=1,
            grid=(count // n,),
            in_specs=[pl.BlockSpec((1, n, 64, 256), lambda s, c: (0, s + skip, 0, 0))] * 2,
            out_specs=pl.BlockSpec((2 * HALF, n, 128), lambda s, c: (0, s, 0)),
            scratch_shapes=[pltpu.VMEM((n * PITCH, 128), jnp.float32)],
        ),
        out_shape=jax.ShapeDtypeStruct((2 * HALF, count, 128), jnp.bfloat16),
        compiler_params=pltpu.CompilerParams(vmem_limit_bytes=48 << 20),
        cost_estimate=pl.CostEstimate(flops=2 * count * 64 * 64 * 256, bytes_accessed=count * 74000, transcendentals=0),
        name="features",
    )(core, g, i)


def wide(ref, first, count):
    return jnp.concatenate([ref[first + t] for t in range(count)], axis=1)


def gram_kernel(pieces, blocks, s_ref, *refs):
    n_in = pieces + 4 + 6 * len(blocks)
    ins, outs = refs[:n_in], refs[n_in : n_in + 4]
    rows, self_cols, side_cols, back_cols, two_cols, sems = refs[n_in + 4 :]
    row_in, own, mate = ins[:pieces], ins[pieces : pieces + 2], ins[pieces + 2 : pieces + 4]
    core = s_ref[5]
    used = iter(range(64))

    def copy(src, dst):
        return pltpu.make_async_copy(src, dst, sems.at[next(used)])

    row_waits, self_waits, side_waits, back_waits, two_waits = [], [], [], [], []
    at = 0
    for piece in row_in:
        size = piece.shape[1]
        moving = copy(piece, rows.at[:, pl.ds(at, size)])
        moving.start()
        row_waits.append(moving)
        at += size
    for k, b in enumerate(blocks):
        side, back, two = (ins[pieces + 4 + 6 * k + 2 * m : pieces + 6 + 6 * k + 2 * m] for m in range(3))
        waits = []
        for p in range(2):
            place = pl.ds(128 * p, 128)
            for h in range(2):
                here = self_cols.at[k, pl.ds(HALF * h, HALF), place]
                sem = sems.at[next(used)]
                mine = pltpu.make_async_copy(own[p].at[pl.ds(HALF * h, HALF)], here, sem)
                theirs = pltpu.make_async_copy(mate[p].at[pl.ds(HALF * (1 - h), HALF)], here, sem)

                @pl.when(core == b)
                def _():
                    mine.start()

                @pl.when(core != b)
                def _():
                    theirs.start()

                waits.append(mine)
        self_waits.append(waits)
        for source, target, group in ((side, side_cols, side_waits), (back, back_cols, back_waits)):
            waits = []
            for p in range(2):
                moving = copy(source[p], target.at[k, :, pl.ds(128 * p, 128)])
                moving.start()
                waits.append(moving)
            group.append(waits)
        waits = []
        for q in range(2):
            for p in range(2):
                moving = copy(two[q].at[p], two_cols.at[k, pl.ds(8 * q, 8), pl.ds(128 * p, 128)])
                moving.start()
                waits.append(moving)
        two_waits.append(waits)

    def finish(waits):
        for moving in waits:
            moving.wait()

    def put(which, k, value):
        for d in range(4):

            @pl.when(s_ref[which] == d)
            def _():
                outs[d][:, 256 * k : 256 * k + 256] = value.astype(outs[d].dtype)

    def dot(left, right):
        return lax.dot_general(left, right, NT, preferred_element_type=jnp.float32)

    finish(row_waits)
    quarter = s_ref[4] * 8
    for k in range(len(blocks)):
        finish(self_waits[k])
        put(0, k, dot(wide(rows, 0, 2 * HALF), wide(self_cols.at[k], 0, 2 * HALF)))
        finish(side_waits[k])
        put(1, k, dot(wide(rows, 0, HALF), wide(side_cols.at[k], 0, HALF)))
        finish(back_waits[k])
        put(2, k, dot(wide(rows, HALF, HALF), wide(back_cols.at[k], 0, HALF)))
        finish(two_waits[k])
        left = jnp.concatenate([wide(rows, quarter, 8), wide(rows, HALF + quarter, 8)], axis=1)
        put(3, k, dot(left, wide(two_cols.at[k], 0, HALF)))


def gram(slots, row_pieces, own, mate, blocks, columns):
    count = sum(piece.shape[1] for piece in row_pieces)
    width = 256 * len(blocks)
    operands = [*row_pieces, *own, *mate]
    for b in blocks:
        operands += columns[b]
    vmem = lambda *shape: pltpu.VMEM(shape, jnp.bfloat16)
    n = len(blocks)
    return pl.pallas_call(
        functools.partial(gram_kernel, len(row_pieces), blocks),
        in_specs=[pl.BlockSpec(memory_space=pltpu.SMEM)] + [pl.BlockSpec(memory_space=pl.ANY)] * len(operands),
        out_specs=[pl.BlockSpec(memory_space=pltpu.VMEM)] * 4,
        out_shape=[jax.ShapeDtypeStruct((count, width), jnp.float32)]
        + [jax.ShapeDtypeStruct((count, width), jnp.bfloat16)] * 3,
        scratch_shapes=[
            vmem(2 * HALF, count, 128),
            vmem(n, 2 * HALF, 256, 128),
            vmem(n, HALF, 256, 128),
            vmem(n, HALF, 256, 128),
            vmem(n, HALF, 256, 128),
            pltpu.SemaphoreType.DMA((len(row_pieces) + 12 * n,)),
        ],
        compiler_params=pltpu.CompilerParams(vmem_limit_bytes=48 << 20),
        cost_estimate=pl.CostEstimate(
            flops=2 * count * width * 10240, bytes_accessed=(5 * n << 20) + count * 8192, transcendentals=0
        ),
        name="gram",
    )(slots, *operands)


def device(x, y, z, c):
    x, y, z = x % 4, y % 4, z % 4
    return ((z * 2 + y // 2) * 2 + c) * 8 + x * 2 + y % 2


def shift(array, move):
    pairs = []
    for x in range(4):
        for y in range(4):
            for z in range(4):
                for c in range(2):
                    place = move(x, y, z, c)
                    if place is not None:
                        pairs.append((device(x, y, z, c), device(*place)))
    return lax.ppermute(array, AXES, pairs)


def other_core(x, y, z, c):
    return x, y, z, 1 - c


def other_half(x, y, z, c):
    return x, y + 2, z, c


def along_z(x, y, z, c):
    return x, y, z - 1 + 2 * c, c


def body(grads_proj, inputs_proj):
    f32, bf16 = jnp.float32, jnp.bfloat16
    dp = lax.axis_index("dp").astype(jnp.int32)
    layer = lax.axis_index("layer").astype(jnp.int32)
    core = dp % 2
    z = dp // 4
    y = (dp // 2) % 2 * 2 + layer % 2
    x = layer // 2
    ordered = lambda here, there: (jnp.where(core == 0, here, there), jnp.where(core == 0, there, here))

    own, far, mate, first, second = [], [], [], [], []
    for p in range(2):
        rows = features(core.reshape(1), grads_proj, inputs_proj, 128 * p, 128)
        own.append(rows)
        far.append(shift(rows, other_half))
        mate.append(shift(rows, other_core))
        a, b = ordered(rows[:HALF], mate[p][HALF:])
        first.append(a)
        second.append(b)
    start = (z - 1 + 2 * core) % 4 // 2 * 8
    columns = []
    for block in (first, second):
        side = [shift(piece, along_z) for piece in block]
        back = [shift(piece, other_core) for piece in side]
        two = shift(jnp.stack([lax.dynamic_slice_in_dim(piece, start, 8, 0) for piece in side]), along_z)
        columns.append([*side, *back, two, shift(two, other_core)])

    near_j = jnp.where(core == 0, 1, 3)
    slots = jnp.stack([z - x, z + near_j - x, z + 4 - near_j - x, z + 2 - x]) % 4
    slots = jnp.concatenate([slots, jnp.stack([z // 2, core])]).astype(jnp.int32)

    def spread(parts):
        return (
            parts[0],
            shift(parts[1], lambda x, y, z, c: (x + 1, y, z, c)),
            shift(parts[2], lambda x, y, z, c: (x + 2, y, z, c)),
            shift(parts[3], lambda x, y, z, c: (x - 1, y, z, c)),
        )

    def add(parts):
        return (parts[0] + parts[1].astype(f32)) + (parts[2].astype(f32) + parts[3].astype(f32))

    early = (own[0], own[1], far[0])
    part_a = gram(slots, early, own, mate, (0,), columns)
    slots, part_a = lax.optimization_barrier((slots, part_a))
    part_b = gram(slots, early, own, mate, (1,), columns)
    slots, part_b = lax.optimization_barrier((slots, part_b))
    part_c = gram(slots, (far[1],), own, mate, (0, 1), columns)
    sum_a, sum_b, sum_c = add(spread(part_a)), add(spread(part_b)), add(spread(part_c))
    both = jnp.concatenate([sum_a, sum_b], axis=1)
    near_sum = both[:256]
    far_sum = jnp.concatenate([both[256:], sum_c], axis=0)

    edge = (y == 0) | (y == 3)
    give = jnp.where(edge, far_sum, near_sum).astype(bf16)
    keep = jnp.where(edge, near_sum, far_sum)
    total = keep + shift(give, lambda x, y, z, c: (x, y ^ 1, z, c)).astype(f32)
    sent = total.astype(bf16)
    direct = shift(sent, lambda x, y, z, c: (x, 3 - y, z, c) if y in (1, 2) else None).astype(f32)
    direct = jnp.where(edge, total, direct)
    same, cross = ordered(sent[:, :256], sent[:, 256:])
    same = shift(same, lambda x, y, z, c: (z, y, x, c) if x != z else None)
    cross = shift(cross, lambda x, y, z, c: (z, y, x, 1 - c) if x != z else None)
    turned = jnp.concatenate(ordered(same.T, cross.T), axis=1).astype(f32)
    return (direct + turned) * (1.0 / (256.0 * jnp.sqrt(f32(8 * 4096))))


def solution(mesh):
    return jax.shard_map(
        body,
        mesh=mesh,
        in_specs=(P("layer", "dp", None, None), P("layer", "dp", None, None)),
        out_specs=P("dp", "layer"),
        check_vma=False,
    )
```

```python
import functools
import jax
import jax.numpy as jnp
from jax import lax
from jax.experimental import pallas as pl
from jax.experimental.pallas import tpu as pltpu
from jax.sharding import PartitionSpec as P

NT = (((1,), (1,)), ((), ()))
AXES = ("dp", "layer")
HALF = 16
QUARTER = 8
PITCH = 68


def feature_kernel(s_ref, g_ref, i_ref, full_ref, *refs):
    pieces, prod = refs[:4], refs[4]
    n = g_ref.shape[1]
    for e in range(0, n, 4):
        four = lax.dot_general(
            g_ref[0, e : e + 4].reshape(256, 256),
            i_ref[0, e : e + 4].reshape(256, 256),
            NT,
            preferred_element_type=jnp.float32,
        )
        for k in range(4):
            prod[pl.ds((e + k) * PITCH, 64), :] = four[64 * k : 64 * k + 64, 128 * (k // 2) : 128 * (k // 2) + 128]
    even = lax.broadcasted_iota(jnp.int32, (n, 128), 0) % 2 == 0
    left = lax.broadcasted_iota(jnp.int32, (n, 128), 1) < 64
    in_place = even == left
    ahead = s_ref[0]
    for k, piece in enumerate(pieces):
        tile = k // 2 * HALF + (ahead if k % 2 == 0 else 1 - ahead) * QUARTER
        for t in range(QUARTER):
            first = prod[pl.ds(2 * tile + 2 * t, n, stride=PITCH), :]
            second = prod[pl.ds(2 * tile + 2 * t + 1, n, stride=PITCH), :]
            moved = pltpu.roll(jnp.where(even, second, first), 64, 1)
            value = jnp.where(in_place, jnp.where(even, first, second), moved).astype(jnp.bfloat16)
            piece[t] = value
            full_ref[tile + t] = value


FREE = pl.CostEstimate(flops=1, bytes_accessed=1, transcendentals=0)
IN_SMEM = pl.BlockSpec(memory_space=pltpu.SMEM)
IN_VMEM = pl.BlockSpec(memory_space=pltpu.VMEM)


def on_chip(*arrays):
    return [pltpu.with_memory_space_constraint(a, pltpu.VMEM) for a in arrays]


def features(ahead, g, i, n=64):
    count = g.shape[1]
    block = lambda tiles: pl.BlockSpec((tiles, n, 128), lambda s, a: (0, s, 0))
    shape = lambda tiles: jax.ShapeDtypeStruct((tiles, count, 128), jnp.bfloat16)
    return pl.pallas_call(
        feature_kernel,
        grid_spec=pltpu.PrefetchScalarGridSpec(
            num_scalar_prefetch=1,
            grid=(count // n,),
            in_specs=[pl.BlockSpec((1, n, 64, 256), lambda s, a: (0, s, 0, 0))] * 2,
            out_specs=[block(2 * HALF)] + [block(QUARTER)] * 4,
            scratch_shapes=[pltpu.VMEM((n * PITCH, 128), jnp.float32)],
        ),
        out_shape=[shape(2 * HALF)] + [shape(QUARTER)] * 4,
        compiler_params=pltpu.CompilerParams(vmem_limit_bytes=24 << 20),
        cost_estimate=FREE,
        name="features",
    )(ahead.reshape(1), *(pltpu.with_memory_space_constraint(a, pltpu.HBM) for a in (g, i)))


def wide(ref, first, count):
    return jnp.concatenate([ref[first + t] for t in range(count)], axis=1)


def gram_kernel(n_rows, s_ref, *refs):
    rows, (own, up_a, up_b, down_a, down_b, two_up, two_down) = refs[:n_rows], refs[n_rows : n_rows + 7]
    outs, slot = refs[-5:-1], refs[-1]

    def dot(left, right):
        return lax.dot_general(left, right, NT, preferred_element_type=jnp.float32)

    def beside(a, b):
        return jnp.concatenate([a, b], axis=1)

    def tall(first, count):
        return jnp.concatenate([wide(part, first, count) for part in rows], axis=0)

    def two_quarters(a, b):
        return beside(tall(a * QUARTER, QUARTER), tall(b * QUARTER, QUARTER))

    def pair(a, b):
        return beside(wide(a, 0, QUARTER), wide(b, 0, QUARTER))

    slot[s_ref[0]] = dot(tall(0, 2 * HALF), wide(own, 0, 2 * HALF))
    slot[s_ref[1]] = dot(two_quarters(s_ref[5], 1 - s_ref[5]), pair(up_a, up_b))
    slot[s_ref[2]] = dot(two_quarters(2 + s_ref[6], 3 - s_ref[6]), pair(down_a, down_b))
    slot[s_ref[3]] = dot(two_quarters(s_ref[4], 2 + s_ref[4]), pair(two_up, two_down))
    for d in range(4):
        outs[d][...] = slot[d].astype(outs[d].dtype)


def gram(scalars, rows, columns):
    count, width = len(rows) * rows[0].shape[1], columns[0].shape[1]
    operands = [*rows, *columns]
    return pl.pallas_call(
        functools.partial(gram_kernel, len(rows)),
        in_specs=[IN_SMEM] + [IN_VMEM] * len(operands),
        out_specs=[IN_VMEM] * 4,
        out_shape=[jax.ShapeDtypeStruct((count, width), jnp.float32)]
        + [jax.ShapeDtypeStruct((count, width), jnp.bfloat16)] * 3,
        scratch_shapes=[pltpu.VMEM((4, count, width), jnp.float32)],
        compiler_params=pltpu.CompilerParams(vmem_limit_bytes=16 << 20),
        cost_estimate=FREE,
        name="gram",
    )(scalars, *on_chip(*operands))


def device(x, y, z, c):
    x, y, z = x % 4, y % 4, z % 4
    return ((z * 2 + y // 2) * 2 + c) * 8 + x * 2 + y % 2


def shift(array, move):
    pairs = []
    for x in range(4):
        for y in range(4):
            for z in range(4):
                for c in range(2):
                    place = move(x, y, z, c)
                    if place is not None:
                        pairs.append((device(x, y, z, c), device(*place)))
    return lax.ppermute(array, AXES, pairs)


def other_core(x, y, z, c):
    return x, y, z, 1 - c


def other_half(x, y, z, c):
    return x, y + 2, z, c


def z_down(x, y, z, c):
    return x, y, z - 1, c


def z_up(x, y, z, c):
    return x, y, z + 1, c


def body(grads_proj, inputs_proj):
    f32, bf16 = jnp.float32, jnp.bfloat16
    after = lax.optimization_barrier
    dp = lax.axis_index("dp").astype(jnp.int32)
    layer = lax.axis_index("layer").astype(jnp.int32)
    core = dp % 2
    z = dp // 4
    y = (dp // 2) % 2 * 2 + layer % 2
    x = layer // 2
    half = lambda at: at % 4 // 2
    scalars = jnp.stack([z - x, z + 1 - x, z + 3 - x, z + 2 - x]) % 4
    scalars = jnp.concatenate([scalars, jnp.stack([half(z), 1 - half(z + 1), 1 - half(z - 1)])]).astype(jnp.int32)

    own, *pieces = features(1 - half(z), grads_proj, inputs_proj)
    up_a, down_a = shift(pieces[0], z_down), shift(pieces[2], z_up)
    up_b, down_b = shift(pieces[1], z_down), shift(pieces[3], z_up)
    mate, far = shift(own, other_core), shift(own, other_half)
    columns = [own, up_a, up_b, down_a, down_b, shift(up_a, z_down), shift(down_a, z_up)]

    def over_x(parts):
        moved = (
            shift(parts[1], lambda x, y, z, c: (x + 1, y, z, c)),
            shift(parts[2], lambda x, y, z, c: (x + 2, y, z, c)),
            shift(parts[3], lambda x, y, z, c: (x - 1, y, z, c)),
        )
        return (parts[0] + moved[0].astype(f32)) + (moved[1].astype(f32) + moved[2].astype(f32))

    near = gram(scalars, [own, mate], columns)
    near, far = after((near, far))
    near_sum = over_x(near)
    far_one = gram(scalars, [far], columns)
    far_mate = shift(far, other_core)
    far_one, far_mate = after((far_one, far_mate))
    far_two = gram(scalars, [far_mate], columns)

    edge = (y == 0) | (y == 3)

    def over_y(near_part, far_part):
        give = jnp.where(edge, far_part, near_part).astype(bf16)
        keep = jnp.where(edge, near_part, far_part)
        return keep + shift(give, lambda x, y, z, c: (x, y ^ 1, z, c)).astype(f32)

    def across(part):
        return shift(part, lambda x, y, z, c: (z, y, x, c) if x != z else None)

    one = over_y(near_sum[:256], over_x(far_one))
    sent_one = one.astype(bf16)
    turn_one = across(sent_one)
    here = shift(sent_one, lambda x, y, z, c: (x, 3 - y, z, c) if y in (1, 2) else None).astype(f32)
    here = jnp.where(edge, one, here)
    two = over_y(near_sum[256:], over_x(far_two))
    sent_two = two.astype(bf16)
    turn_two = across(sent_two)
    there = shift(sent_two, lambda x, y, z, c: (x, 3 - y if y in (1, 2) else y, z, 1 - c)).astype(f32)
    here = here + turn_one.T.astype(f32)
    there = there + turn_two.T.astype(f32)
    out = jnp.concatenate([jnp.where(core == 0, here, there), jnp.where(core == 0, there, here)], axis=1)
    return out * (1.0 / (256.0 * jnp.sqrt(f32(8 * 4096))))


def solution(mesh):
    return jax.shard_map(
        body,
        mesh=mesh,
        in_specs=(P("layer", "dp", None, None), P("layer", "dp", None, None)),
        out_specs=P("dp", "layer"),
        check_vma=False,
    )
```

```python
import functools
import jax
import jax.numpy as jnp
from jax import lax
from jax.experimental import pallas as pl
from jax.experimental.pallas import tpu as pltpu
from jax.sharding import PartitionSpec as P

NT = (((1,), (1,)), ((), ()))
AXES = ("dp", "layer")
HALF = 16
QUARTER = 8
PITCH = 68


def feature_kernel(s_ref, g_ref, i_ref, full_ref, *refs):
    pieces, prod = refs[:4], refs[4]
    n = g_ref.shape[1]
    for e in range(0, n, 4):
        four = lax.dot_general(
            g_ref[0, e : e + 4].reshape(256, 256),
            i_ref[0, e : e + 4].reshape(256, 256),
            NT,
            preferred_element_type=jnp.float32,
        )
        for k in range(4):
            prod[pl.ds((e + k) * PITCH, 64), :] = four[64 * k : 64 * k + 64, 128 * (k // 2) : 128 * (k // 2) + 128]
    even = lax.broadcasted_iota(jnp.int32, (n, 128), 0) % 2 == 0
    left = lax.broadcasted_iota(jnp.int32, (n, 128), 1) < 64
    in_place = even == left
    ahead = s_ref[0]
    for k, piece in enumerate(pieces):
        tile = k // 2 * HALF + (ahead if k % 2 == 0 else 1 - ahead) * QUARTER
        for t in range(QUARTER):
            first = prod[pl.ds(2 * tile + 2 * t, n, stride=PITCH), :]
            second = prod[pl.ds(2 * tile + 2 * t + 1, n, stride=PITCH), :]
            moved = pltpu.roll(jnp.where(even, second, first), 64, 1)
            value = jnp.where(in_place, jnp.where(even, first, second), moved).astype(jnp.bfloat16)
            piece[t] = value
            full_ref[tile + t] = value


FREE = pl.CostEstimate(flops=1, bytes_accessed=1, transcendentals=0)
IN_SMEM = pl.BlockSpec(memory_space=pltpu.SMEM)
IN_VMEM = pl.BlockSpec(memory_space=pltpu.VMEM)


def on_chip(*arrays):
    return [pltpu.with_memory_space_constraint(a, pltpu.VMEM) for a in arrays]


def features(ahead, g, i, n=64):
    count = g.shape[1]
    block = lambda tiles: pl.BlockSpec((tiles, n, 128), lambda s, a: (0, s, 0))
    shape = lambda tiles: jax.ShapeDtypeStruct((tiles, count, 128), jnp.bfloat16)
    return pl.pallas_call(
        feature_kernel,
        grid_spec=pltpu.PrefetchScalarGridSpec(
            num_scalar_prefetch=1,
            grid=(count // n,),
            in_specs=[pl.BlockSpec((1, n, 64, 256), lambda s, a: (0, s, 0, 0))] * 2,
            out_specs=[block(2 * HALF)] + [block(QUARTER)] * 4,
            scratch_shapes=[pltpu.VMEM((n * PITCH, 128), jnp.float32)],
        ),
        out_shape=[shape(2 * HALF)] + [shape(QUARTER)] * 4,
        compiler_params=pltpu.CompilerParams(vmem_limit_bytes=24 << 20),
        cost_estimate=FREE,
        name="features",
    )(ahead.reshape(1), *(pltpu.with_memory_space_constraint(a, pltpu.HBM) for a in (g, i)))


def wide(ref, first, count):
    return jnp.concatenate([ref[first + t] for t in range(count)], axis=1)


def gram_kernel(n_rows, s_ref, *refs):
    rows, (own, up_a, up_b, down_a, down_b, two_up, two_down) = refs[:n_rows], refs[n_rows : n_rows + 7]
    outs, slot = refs[-5:-1], refs[-1]

    def dot(left, right):
        return lax.dot_general(left, right, NT, preferred_element_type=jnp.float32)

    def beside(a, b):
        return jnp.concatenate([a, b], axis=1)

    def tall(first, count):
        return jnp.concatenate([wide(part, first, count) for part in rows], axis=0)

    def two_quarters(a, b):
        return beside(tall(a * QUARTER, QUARTER), tall(b * QUARTER, QUARTER))

    def pair(a, b):
        return beside(wide(a, 0, QUARTER), wide(b, 0, QUARTER))

    slot[s_ref[0]] = dot(tall(0, 2 * HALF), wide(own, 0, 2 * HALF))
    slot[s_ref[1]] = dot(two_quarters(s_ref[5], 1 - s_ref[5]), pair(up_a, up_b))
    slot[s_ref[2]] = dot(two_quarters(2 + s_ref[6], 3 - s_ref[6]), pair(down_a, down_b))
    slot[s_ref[3]] = dot(two_quarters(s_ref[4], 2 + s_ref[4]), pair(two_up, two_down))
    for d in range(4):
        outs[d][...] = slot[d].astype(outs[d].dtype)


def gram(scalars, rows, columns):
    count, width = len(rows) * rows[0].shape[1], columns[0].shape[1]
    operands = [*rows, *columns]
    return pl.pallas_call(
        functools.partial(gram_kernel, len(rows)),
        in_specs=[IN_SMEM] + [IN_VMEM] * len(operands),
        out_specs=[IN_VMEM] * 4,
        out_shape=[jax.ShapeDtypeStruct((count, width), jnp.float32)]
        + [jax.ShapeDtypeStruct((count, width), jnp.bfloat16)] * 3,
        scratch_shapes=[pltpu.VMEM((4, count, width), jnp.float32)],
        compiler_params=pltpu.CompilerParams(vmem_limit_bytes=16 << 20),
        cost_estimate=FREE,
        name="gram",
    )(scalars, *on_chip(*operands))


def device(x, y, z, c):
    x, y, z = x % 4, y % 4, z % 4
    return ((z * 2 + y // 2) * 2 + c) * 8 + x * 2 + y % 2


def shift(array, move):
    pairs = []
    for x in range(4):
        for y in range(4):
            for z in range(4):
                for c in range(2):
                    place = move(x, y, z, c)
                    if place is not None:
                        pairs.append((device(x, y, z, c), device(*place)))
    return lax.ppermute(array, AXES, pairs)


def other_core(x, y, z, c):
    return x, y, z, 1 - c


def other_half(x, y, z, c):
    return x, y + 2, z, c


def z_down(x, y, z, c):
    return x, y, z - 1, c


def z_up(x, y, z, c):
    return x, y, z + 1, c


def body(grads_proj, inputs_proj):
    f32, bf16 = jnp.float32, jnp.bfloat16
    after = lax.optimization_barrier
    dp = lax.axis_index("dp").astype(jnp.int32)
    layer = lax.axis_index("layer").astype(jnp.int32)
    core = dp % 2
    z = dp // 4
    y = (dp // 2) % 2 * 2 + layer % 2
    x = layer // 2
    half = lambda at: at % 4 // 2
    scalars = jnp.stack([z - x, z + 1 - x, z + 3 - x, z + 2 - x]) % 4
    scalars = jnp.concatenate([scalars, jnp.stack([half(z), 1 - half(z + 1), 1 - half(z - 1)])]).astype(jnp.int32)

    own, *pieces = features(1 - half(z), grads_proj, inputs_proj)
    up_a, down_a = shift(pieces[0], z_down), shift(pieces[2], z_up)
    mate, far = shift(own, other_core), shift(own, other_half)
    mate, *later = after((mate, pieces[1], pieces[3]))
    up_b, down_b = shift(later[0], z_down), shift(later[1], z_up)
    columns = [own, up_a, up_b, down_a, down_b, shift(up_a, z_down), shift(down_a, z_up)]

    def over_x(parts):
        moved = (
            shift(parts[1], lambda x, y, z, c: (x + 1, y, z, c)),
            shift(parts[2], lambda x, y, z, c: (x + 2, y, z, c)),
            shift(parts[3], lambda x, y, z, c: (x - 1, y, z, c)),
        )
        return (parts[0] + moved[0].astype(f32)) + (moved[1].astype(f32) + moved[2].astype(f32))

    near = gram(scalars, [own, mate], columns)
    near, far = after((near, far))
    near_sum = over_x(near)
    far_one = gram(scalars, [far], columns)
    far_mate = shift(far, other_core)
    far_one, far_mate = after((far_one, far_mate))
    far_two = gram(scalars, [far_mate], columns)

    edge = (y == 0) | (y == 3)

    def over_y(near_part, far_part):
        give = jnp.where(edge, far_part, near_part).astype(bf16)
        keep = jnp.where(edge, near_part, far_part)
        return keep + shift(give, lambda x, y, z, c: (x, y ^ 1, z, c)).astype(f32)

    def across(part):
        return shift(part, lambda x, y, z, c: (z, y, x, c) if x != z else None)

    one = over_y(near_sum[:256], over_x(far_one))
    sent_one = one.astype(bf16)
    turn_one = across(sent_one)
    here = shift(sent_one, lambda x, y, z, c: (x, 3 - y, z, c) if y in (1, 2) else None).astype(f32)
    here = jnp.where(edge, one, here)
    one_done, far_two = after((one, over_x(far_two)))
    two = over_y(near_sum[256:], far_two)
    sent_two = two.astype(bf16)
    turn_two = across(sent_two)
    there = shift(sent_two, lambda x, y, z, c: (x, 3 - y if y in (1, 2) else y, z, 1 - c)).astype(f32)
    here = here + turn_one.T.astype(f32)
    there = there + turn_two.T.astype(f32)
    out = jnp.concatenate([jnp.where(core == 0, here, there), jnp.where(core == 0, there, here)], axis=1)
    return out * (1.0 / (256.0 * jnp.sqrt(f32(8 * 4096))))


def solution(mesh):
    return jax.shard_map(
        body,
        mesh=mesh,
        in_specs=(P("layer", "dp", None, None), P("layer", "dp", None, None)),
        out_specs=P("dp", "layer"),
        check_vma=False,
    )
```

```python
import functools
import jax
import jax.numpy as jnp
from jax import lax
from jax.experimental import pallas as pl
from jax.experimental.pallas import tpu as pltpu
from jax.sharding import PartitionSpec as P

NT = (((1,), (1,)), ((), ()))
AXES = ("dp", "layer")
HALF = 16
QUARTER = 8
PITCH = 68


def feature_kernel(s_ref, g_ref, i_ref, full_ref, *refs):
    pieces, prod = refs[:4], refs[4]
    n = g_ref.shape[1]
    for e in range(0, n, 4):
        four = lax.dot_general(
            g_ref[0, e : e + 4].reshape(256, 256),
            i_ref[0, e : e + 4].reshape(256, 256),
            NT,
            preferred_element_type=jnp.float32,
        )
        for k in range(4):
            prod[pl.ds((e + k) * PITCH, 64), :] = four[64 * k : 64 * k + 64, 128 * (k // 2) : 128 * (k // 2) + 128]
    even = lax.broadcasted_iota(jnp.int32, (n, 128), 0) % 2 == 0
    left = lax.broadcasted_iota(jnp.int32, (n, 128), 1) < 64
    in_place = even == left
    ahead = s_ref[0]
    for k, piece in enumerate(pieces):
        tile = k // 2 * HALF + (ahead if k % 2 == 0 else 1 - ahead) * QUARTER
        for t in range(QUARTER):
            first = prod[pl.ds(2 * tile + 2 * t, n, stride=PITCH), :]
            second = prod[pl.ds(2 * tile + 2 * t + 1, n, stride=PITCH), :]
            moved = pltpu.roll(jnp.where(even, second, first), 64, 1)
            value = jnp.where(in_place, jnp.where(even, first, second), moved).astype(jnp.bfloat16)
            piece[t] = value
            full_ref[tile + t] = value


FREE = pl.CostEstimate(flops=1, bytes_accessed=1, transcendentals=0)
IN_SMEM = pl.BlockSpec(memory_space=pltpu.SMEM)
IN_VMEM = pl.BlockSpec(memory_space=pltpu.VMEM)


def on_chip(*arrays):
    return [pltpu.with_memory_space_constraint(a, pltpu.VMEM) for a in arrays]


def features(ahead, g, i, n=64):
    count = g.shape[1]
    block = lambda tiles: pl.BlockSpec((tiles, n, 128), lambda s, a: (0, s, 0))
    shape = lambda tiles: jax.ShapeDtypeStruct((tiles, count, 128), jnp.bfloat16)
    return pl.pallas_call(
        feature_kernel,
        grid_spec=pltpu.PrefetchScalarGridSpec(
            num_scalar_prefetch=1,
            grid=(count // n,),
            in_specs=[pl.BlockSpec((1, n, 64, 256), lambda s, a: (0, s, 0, 0))] * 2,
            out_specs=[block(2 * HALF)] + [block(QUARTER)] * 4,
            scratch_shapes=[pltpu.VMEM((n * PITCH, 128), jnp.float32)],
        ),
        out_shape=[shape(2 * HALF)] + [shape(QUARTER)] * 4,
        compiler_params=pltpu.CompilerParams(vmem_limit_bytes=24 << 20),
        cost_estimate=FREE,
        name="features",
    )(ahead.reshape(1), *(pltpu.with_memory_space_constraint(a, pltpu.HBM) for a in (g, i)))


def wide(ref, first, count):
    return jnp.concatenate([ref[first + t] for t in range(count)], axis=1)


def gram_kernel(n_rows, s_ref, *refs):
    rows, (own, up_a, up_b, down_a, down_b, two_up, two_down) = refs[:n_rows], refs[n_rows : n_rows + 7]
    outs, slot = refs[-5:-1], refs[-1]

    def dot(left, right):
        return lax.dot_general(left, right, NT, preferred_element_type=jnp.float32)

    def beside(a, b):
        return jnp.concatenate([a, b], axis=1)

    def tall(first, count):
        return jnp.concatenate([wide(part, first, count) for part in rows], axis=0)

    def two_quarters(a, b):
        return beside(tall(a * QUARTER, QUARTER), tall(b * QUARTER, QUARTER))

    def pair(a, b):
        return beside(wide(a, 0, QUARTER), wide(b, 0, QUARTER))

    slot[s_ref[0]] = dot(tall(0, 2 * HALF), wide(own, 0, 2 * HALF))
    slot[s_ref[1]] = dot(two_quarters(s_ref[5], 1 - s_ref[5]), pair(up_a, up_b))
    slot[s_ref[2]] = dot(two_quarters(2 + s_ref[6], 3 - s_ref[6]), pair(down_a, down_b))
    slot[s_ref[3]] = dot(two_quarters(s_ref[4], 2 + s_ref[4]), pair(two_up, two_down))
    for d in range(4):
        outs[d][...] = slot[d].astype(outs[d].dtype)


def gram(scalars, rows, columns):
    count, width = len(rows) * rows[0].shape[1], columns[0].shape[1]
    operands = [*rows, *columns]
    return pl.pallas_call(
        functools.partial(gram_kernel, len(rows)),
        in_specs=[IN_SMEM] + [IN_VMEM] * len(operands),
        out_specs=[IN_VMEM] * 4,
        out_shape=[jax.ShapeDtypeStruct((count, width), jnp.float32)]
        + [jax.ShapeDtypeStruct((count, width), jnp.bfloat16)] * 3,
        scratch_shapes=[pltpu.VMEM((4, count, width), jnp.float32)],
        compiler_params=pltpu.CompilerParams(vmem_limit_bytes=16 << 20),
        cost_estimate=FREE,
        name="gram",
    )(scalars, *on_chip(*operands))


def device(x, y, z, c):
    x, y, z = x % 4, y % 4, z % 4
    return ((z * 2 + y // 2) * 2 + c) * 8 + x * 2 + y % 2


def shift(array, move):
    pairs = []
    for x in range(4):
        for y in range(4):
            for z in range(4):
                for c in range(2):
                    place = move(x, y, z, c)
                    if place is not None:
                        pairs.append((device(x, y, z, c), device(*place)))
    return lax.ppermute(array, AXES, pairs)


def other_core(x, y, z, c):
    return x, y, z, 1 - c


def other_half(x, y, z, c):
    return x, y + 2, z, c


def z_down(x, y, z, c):
    return x, y, z - 1, c


def z_up(x, y, z, c):
    return x, y, z + 1, c


def body(grads_proj, inputs_proj):
    f32, bf16 = jnp.float32, jnp.bfloat16
    after = lax.optimization_barrier
    dp = lax.axis_index("dp").astype(jnp.int32)
    layer = lax.axis_index("layer").astype(jnp.int32)
    core = dp % 2
    z = dp // 4
    y = (dp // 2) % 2 * 2 + layer % 2
    x = layer // 2
    half = lambda at: at % 4 // 2
    scalars = jnp.stack([z - x, z + 1 - x, z + 3 - x, z + 2 - x]) % 4
    scalars = jnp.concatenate([scalars, jnp.stack([half(z), 1 - half(z + 1), 1 - half(z - 1)])]).astype(jnp.int32)

    own, *pieces = features(1 - half(z), grads_proj, inputs_proj)
    up_a, down_a = shift(pieces[0], z_down), shift(pieces[2], z_up)
    up_b, down_b = shift(pieces[1], z_down), shift(pieces[3], z_up)
    mate, far = shift(own, other_core), shift(own, other_half)
    columns = [own, up_a, up_b, down_a, down_b, shift(up_a, z_down), shift(down_a, z_up)]

    def over_x(parts):
        moved = (
            shift(parts[1], lambda x, y, z, c: (x + 1, y, z, c)),
            shift(parts[2], lambda x, y, z, c: (x + 2, y, z, c)),
            shift(parts[3], lambda x, y, z, c: (x - 1, y, z, c)),
        )
        return (parts[0] + moved[0].astype(f32)) + (moved[1].astype(f32) + moved[2].astype(f32))

    near = gram(scalars, [own, mate], columns)
    near, far = after((near, far))
    near_sum = over_x(near)
    far_one = gram(scalars, [far], columns)
    far_mate = shift(far, other_core)
    far_one, far_mate = after((far_one, far_mate))
    far_two = gram(scalars, [far_mate], columns)

    edge = (y == 0) | (y == 3)

    def over_y(near_part, far_part):
        give = jnp.where(edge, far_part, near_part).astype(bf16)
        keep = jnp.where(edge, near_part, far_part)
        return keep + shift(give, lambda x, y, z, c: (x, y ^ 1, z, c)).astype(f32)

    def across(part):
        return shift(part, lambda x, y, z, c: (z, y, x, c) if x != z else None)

    one = over_y(near_sum[:256], over_x(far_one))
    sent_one = one.astype(bf16)
    turn_one = across(sent_one)
    here = shift(sent_one, lambda x, y, z, c: (x, 3 - y, z, c) if y in (1, 2) else None).astype(f32)
    here = jnp.where(edge, one, here)
    _, far_two = after((one, over_x(far_two)))
    two = over_y(near_sum[256:], far_two)
    sent_two = two.astype(bf16)
    turn_two = across(sent_two)
    there = shift(sent_two, lambda x, y, z, c: (x, 3 - y if y in (1, 2) else y, z, 1 - c)).astype(f32)
    here = here + turn_one.T.astype(f32)
    there = there + turn_two.T.astype(f32)
    out = jnp.concatenate([jnp.where(core == 0, here, there), jnp.where(core == 0, there, here)], axis=1)
    return out * (1.0 / (256.0 * jnp.sqrt(f32(8 * 4096))))


def solution(mesh):
    return jax.shard_map(
        body,
        mesh=mesh,
        in_specs=(P("layer", "dp", None, None), P("layer", "dp", None, None)),
        out_specs=P("dp", "layer"),
        check_vma=False,
    )
```

```python
import functools
import jax
import jax.numpy as jnp
from jax import lax
from jax.experimental import pallas as pl
from jax.experimental.pallas import tpu as pltpu
from jax.sharding import PartitionSpec as P

NT = (((1,), (1,)), ((), ()))
AXES = ("dp", "layer")
HALF = 16
QUARTER = 8
PITCH = 68


def feature_kernel(s_ref, g_ref, i_ref, full_ref, *refs):
    pieces, prod = refs[:4], refs[4]
    n = g_ref.shape[1]
    for e in range(0, n, 4):
        four = lax.dot_general(
            g_ref[0, e : e + 4].reshape(256, 256),
            i_ref[0, e : e + 4].reshape(256, 256),
            NT,
            preferred_element_type=jnp.float32,
        )
        for k in range(4):
            prod[pl.ds((e + k) * PITCH, 64), :] = four[64 * k : 64 * k + 64, 128 * (k // 2) : 128 * (k // 2) + 128]
    even = lax.broadcasted_iota(jnp.int32, (n, 128), 0) % 2 == 0
    left = lax.broadcasted_iota(jnp.int32, (n, 128), 1) < 64
    in_place = even == left
    ahead = s_ref[0]
    for k, piece in enumerate(pieces):
        tile = k // 2 * HALF + (ahead if k % 2 == 0 else 1 - ahead) * QUARTER
        for t in range(QUARTER):
            first = prod[pl.ds(2 * tile + 2 * t, n, stride=PITCH), :]
            second = prod[pl.ds(2 * tile + 2 * t + 1, n, stride=PITCH), :]
            moved = pltpu.roll(jnp.where(even, second, first), 64, 1)
            value = jnp.where(in_place, jnp.where(even, first, second), moved).astype(jnp.bfloat16)
            piece[t] = value
            full_ref[tile + t] = value


FREE = pl.CostEstimate(flops=1, bytes_accessed=1, transcendentals=0)
IN_SMEM = pl.BlockSpec(memory_space=pltpu.SMEM)
IN_VMEM = pl.BlockSpec(memory_space=pltpu.VMEM)


def on_chip(*arrays):
    return [pltpu.with_memory_space_constraint(a, pltpu.VMEM) for a in arrays]


def features(ahead, g, i, n=64):
    count = g.shape[1]
    block = lambda tiles: pl.BlockSpec((tiles, n, 128), lambda s, a: (0, s, 0))
    shape = lambda tiles: jax.ShapeDtypeStruct((tiles, count, 128), jnp.bfloat16)
    return pl.pallas_call(
        feature_kernel,
        grid_spec=pltpu.PrefetchScalarGridSpec(
            num_scalar_prefetch=1,
            grid=(count // n,),
            in_specs=[pl.BlockSpec((1, n, 64, 256), lambda s, a: (0, s, 0, 0))] * 2,
            out_specs=[block(2 * HALF)] + [block(QUARTER)] * 4,
            scratch_shapes=[pltpu.VMEM((n * PITCH, 128), jnp.float32)],
        ),
        out_shape=[shape(2 * HALF)] + [shape(QUARTER)] * 4,
        compiler_params=pltpu.CompilerParams(vmem_limit_bytes=24 << 20),
        cost_estimate=FREE,
        name="features",
    )(ahead.reshape(1), *(pltpu.with_memory_space_constraint(a, pltpu.HBM) for a in (g, i)))


def wide(ref, first, count):
    return jnp.concatenate([ref[first + t] for t in range(count)], axis=1)


def gram_kernel(n_rows, s_ref, *refs):
    rows, (own, up_a, up_b, down_a, down_b, two_up, two_down) = refs[:n_rows], refs[n_rows : n_rows + 7]
    outs, slot = refs[-5:-1], refs[-1]

    def dot(left, right):
        return lax.dot_general(left, right, NT, preferred_element_type=jnp.float32)

    def beside(a, b):
        return jnp.concatenate([a, b], axis=1)

    def tall(first, count):
        return jnp.concatenate([wide(part, first, count) for part in rows], axis=0)

    def two_quarters(a, b):
        return beside(tall(a * QUARTER, QUARTER), tall(b * QUARTER, QUARTER))

    def pair(a, b):
        return beside(wide(a, 0, QUARTER), wide(b, 0, QUARTER))

    slot[s_ref[0]] = dot(tall(0, 2 * HALF), wide(own, 0, 2 * HALF))
    slot[s_ref[1]] = dot(two_quarters(s_ref[5], 1 - s_ref[5]), pair(up_a, up_b))
    slot[s_ref[2]] = dot(two_quarters(2 + s_ref[6], 3 - s_ref[6]), pair(down_a, down_b))
    slot[s_ref[3]] = dot(two_quarters(s_ref[4], 2 + s_ref[4]), pair(two_up, two_down))
    for d in range(4):
        outs[d][...] = slot[d].astype(outs[d].dtype)


def gram(scalars, rows, columns):
    count, width = len(rows) * rows[0].shape[1], columns[0].shape[1]
    operands = [*rows, *columns]
    return pl.pallas_call(
        functools.partial(gram_kernel, len(rows)),
        in_specs=[IN_SMEM] + [IN_VMEM] * len(operands),
        out_specs=[IN_VMEM] * 4,
        out_shape=[jax.ShapeDtypeStruct((count, width), jnp.float32)]
        + [jax.ShapeDtypeStruct((count, width), jnp.bfloat16)] * 3,
        scratch_shapes=[pltpu.VMEM((4, count, width), jnp.float32)],
        compiler_params=pltpu.CompilerParams(vmem_limit_bytes=16 << 20),
        cost_estimate=FREE,
        name="gram",
    )(scalars, *on_chip(*operands))


def device(x, y, z, c):
    x, y, z = x % 4, y % 4, z % 4
    return ((z * 2 + y // 2) * 2 + c) * 8 + x * 2 + y % 2


def shift(array, move):
    pairs = []
    for x in range(4):
        for y in range(4):
            for z in range(4):
                for c in range(2):
                    place = move(x, y, z, c)
                    if place is not None:
                        pairs.append((device(x, y, z, c), device(*place)))
    return lax.ppermute(array, AXES, pairs)


def other_core(x, y, z, c):
    return x, y, z, 1 - c


def other_half(x, y, z, c):
    return x, y + 2, z, c


def z_down(x, y, z, c):
    return x, y, z - 1, c


def z_up(x, y, z, c):
    return x, y, z + 1, c


def body(grads_proj, inputs_proj):
    f32, bf16 = jnp.float32, jnp.bfloat16
    after = lax.optimization_barrier
    dp = lax.axis_index("dp").astype(jnp.int32)
    layer = lax.axis_index("layer").astype(jnp.int32)
    core = dp % 2
    z = dp // 4
    y = (dp // 2) % 2 * 2 + layer % 2
    x = layer // 2
    half = lambda at: at % 4 // 2
    scalars = jnp.stack([z - x, z + 1 - x, z + 3 - x, z + 2 - x]) % 4
    scalars = jnp.concatenate([scalars, jnp.stack([half(z), 1 - half(z + 1), 1 - half(z - 1)])]).astype(jnp.int32)

    own, *pieces = features(1 - half(z), grads_proj, inputs_proj)
    up_a, down_a = shift(pieces[0], z_down), shift(pieces[2], z_up)
    up_b, down_b = shift(pieces[1], z_down), shift(pieces[3], z_up)
    mate, far = shift(own, other_core), shift(own, other_half)
    columns = [own, up_a, up_b, down_a, down_b, shift(up_a, z_down), shift(down_a, z_up)]

    def to_x(parts):
        return [
            shift(parts[1], lambda x, y, z, c: (x + 1, y, z, c)),
            shift(parts[2], lambda x, y, z, c: (x + 2, y, z, c)),
            shift(parts[3], lambda x, y, z, c: (x - 1, y, z, c)),
        ]

    def over_x(parts, moved=None):
        moved = to_x(parts) if moved is None else moved
        return (parts[0] + moved[0].astype(f32)) + (moved[1].astype(f32) + moved[2].astype(f32))

    near = gram(scalars, [own, mate], columns)
    moved = to_x(near)
    far, _ = after((far, near[0]))
    near_sum = over_x(near, moved)
    far_one = gram(scalars, [far], columns)
    far_then, _ = after((far, moved[0]))
    far_mate = shift(far_then, other_core)
    late, _ = after((scalars, far_one[0]))
    far_two = gram(late, [far_mate], columns)

    edge = (y == 0) | (y == 3)

    def over_y(near_part, far_part):
        give = jnp.where(edge, far_part, near_part).astype(bf16)
        keep = jnp.where(edge, near_part, far_part)
        return keep + shift(give, lambda x, y, z, c: (x, y ^ 1, z, c)).astype(f32)

    def across(part):
        return shift(part, lambda x, y, z, c: (z, y, x, c) if x != z else None)

    one = over_y(near_sum[:256], over_x(far_one))
    sent_one = one.astype(bf16)
    turn_one = across(sent_one)
    here = shift(sent_one, lambda x, y, z, c: (x, 3 - y, z, c) if y in (1, 2) else None).astype(f32)
    here = jnp.where(edge, one, here)
    _, far_two = after((one, over_x(far_two)))
    two = over_y(near_sum[256:], far_two)
    sent_two = two.astype(bf16)
    turn_two = across(sent_two)
    there = shift(sent_two, lambda x, y, z, c: (x, 3 - y if y in (1, 2) else y, z, 1 - c)).astype(f32)
    here = here + turn_one.T.astype(f32)
    there = there + turn_two.T.astype(f32)
    out = jnp.concatenate([jnp.where(core == 0, here, there), jnp.where(core == 0, there, here)], axis=1)
    return out * (1.0 / (256.0 * jnp.sqrt(f32(8 * 4096))))


def solution(mesh):
    return jax.shard_map(
        body,
        mesh=mesh,
        in_specs=(P("layer", "dp", None, None), P("layer", "dp", None, None)),
        out_specs=P("dp", "layer"),
        check_vma=False,
    )
```
